32 devices in a mesh: grp: 2 (over x), tm: 16 (over z, y, core).
Axes of the slice: x: 2, y: 2, z: 4, core: 2. Of those that a mesh axis runs over, the one named last changes fastest.
Arguments:
- waveform: float32 [262144], P(('grp', 'tm')), parts along dimension 0, may hold values from -8 to 8
- enc_weight: float32 [16, 256], replicated, may hold values from -1.5 to 1.5
- intra_qkv: bfloat16 [256, 768], replicated, may hold values from -3 to 3
- intra_out: bfloat16 [256, 256], replicated, may hold values from -0.375 to 0.375
- intra_up: bfloat16 [256, 1024], replicated, may hold values from -0.375 to 0.375
- intra_down: bfloat16 [1024, 256], replicated, may hold values from -0.1875 to 0.1875
- inter_qkv: bfloat16 [256, 768], replicated, may hold values from -3 to 3
- inter_out: bfloat16 [256, 256], replicated, may hold values from -0.375 to 0.375
- inter_up: bfloat16 [256, 1024], replicated, may hold values from -0.375 to 0.375
- inter_down: bfloat16 [1024, 256], replicated, may hold values from -0.1875 to 0.1875
- mask_weight: bfloat16 [256, 512], replicated, may hold values from -0.375 to 0.375
Outputs:
- separated: bfloat16 [2, 32768, 256], P(None, ('grp', 'tm')), parts along dimension 1
The draws below stay inside these ranges and needn't reach their ends.
There are 2 independent parts, one for each index of `grp`. The reference program is written for one: setup_inputs(seed, part) draws one part's arguments, and reference() takes and returns one part's arrays. A program takes and returns all parts, laid end to end along the dimension named above; an argument that names none is the same for every part. Nothing has to cross between parts.
All inputs are finite; a program needn't handle non-finite values.
Results may differ from the reference program's by a relative error of at most 0.011.
Values may be sent and summed in bfloat16 or wider, within the bound.
A program may use at most 192 MiB of HBM per device.

```python
import math
import jax
import jax.numpy as jnp
from jax import lax

D = 256
HEADS = 8
HEAD = 32
FFN = 1024
TAPS = 16
HOP = 8
HALF = 128
FRAMES = 16384
SAMPLES = 131072
SEGMENTS = 128


def draw_waveform(key, part):
    key_noise, key_level = jax.random.split(key)
    levels = jnp.exp(jax.random.uniform(key_level, (SAMPLES // 256,), jnp.float32, -1.5, 1.5))
    noise = jax.random.normal(key_noise, (SAMPLES // 256, 256), jnp.float32)
    return jnp.clip(noise * levels[:, None], -8.0, 8.0).reshape(SAMPLES)


def draw_projection(key, model_width):
    key_main = jax.random.fold_in(key, 0)
    noise = jax.random.normal(key_main, (model_width, 3 * model_width), jnp.float32) / math.sqrt(model_width)
    result = noise
    return jnp.clip(result, -3.0, 3.0)


def draw_intra_qkv(key, part):
    return draw_projection(jax.random.fold_in(key, 11), D).astype(jnp.bfloat16)


def draw_inter_qkv(key, part):
    return draw_projection(jax.random.fold_in(key, 23), D).astype(jnp.bfloat16)


def bell_draw(rng, dims, width, limit, held_as=jnp.bfloat16):
    return jnp.clip(width * jax.random.normal(rng, dims, jnp.float32), -limit, limit).astype(held_as)


def setup_inputs(seed: int = 0, part: int = 0) -> dict:
    keys = jax.random.split(jax.random.key(seed), 12)
    own_keys = jax.random.split(jax.random.fold_in(keys[11], part), 12)
    waveform = draw_waveform(jax.random.fold_in(jax.random.fold_in(keys[11], part), 71), part)
    enc_weight = bell_draw(keys[1], (TAPS, D), TAPS ** -0.5, 1.5, jnp.float32)
    intra_qkv = draw_intra_qkv(jax.random.fold_in(keys[11], 71), part)
    intra_out = bell_draw(keys[3], (D, D), D ** -0.5, 0.375)
    intra_up = bell_draw(keys[4], (D, FFN), D ** -0.5, 0.375)
    intra_down = bell_draw(keys[5], (FFN, D), FFN ** -0.5, 0.1875)
    inter_qkv = draw_inter_qkv(jax.random.fold_in(keys[11], 71), part)
    inter_out = bell_draw(keys[7], (D, D), D ** -0.5, 0.375)
    inter_up = bell_draw(keys[8], (D, FFN), D ** -0.5, 0.375)
    inter_down = bell_draw(keys[9], (FFN, D), FFN ** -0.5, 0.1875)
    mask_weight = bell_draw(keys[10], (D, 2 * D), D ** -0.5, 0.375)
    return {"waveform": waveform, "enc_weight": enc_weight, "intra_qkv": intra_qkv, "intra_out": intra_out, "intra_up": intra_up, "intra_down": intra_down, "inter_qkv": inter_qkv, "inter_out": inter_out, "inter_up": inter_up, "inter_down": inter_down, "mask_weight": mask_weight}


def rounded(values):
    return lax.optimization_barrier(values.astype(jnp.bfloat16))

def layer_norm(values):
    values = values.astype(jnp.float32)
    centred = values - lax.optimization_barrier(jnp.mean(values, axis=-1, keepdims=True))
    spread = lax.optimization_barrier(jnp.mean(centred * centred, axis=-1, keepdims=True))
    return centred * lax.rsqrt(spread + 1e-05)

def project(values, weight):
    flattened = values.reshape(-1, values.shape[-1])
    result = jnp.dot(flattened, weight, preferred_element_type=jnp.float32)
    return result.reshape(values.shape[:-1] + (weight.shape[1],))

def attend(queries, key_rows, value_rows, seq_first):
    full_shape = queries.shape
    split_shape = full_shape[:-1] + (HEADS, HEAD)
    query_heads = queries.reshape(split_shape).astype(jnp.float32)
    key_heads = key_rows.reshape(split_shape).astype(jnp.float32)
    value_heads = value_rows.reshape(split_shape).astype(jnp.float32)
    if seq_first:
        score_form = 'lbhe,kbhe->bhlk'
        weigh_form = 'bhlk,kbhe->lbhe'
    else:
        score_form = 'blhe,bkhe->bhlk'
        weigh_form = 'bhlk,bkhe->blhe'
    scores = jnp.einsum(score_form, query_heads, key_heads) * HEAD ** (-0.5)
    probs = jax.nn.softmax(scores, axis=-1).astype(jnp.bfloat16)
    mixture = jnp.einsum(weigh_form, probs.astype(jnp.float32), value_heads)
    return mixture.astype(jnp.bfloat16).reshape(full_shape)

def transformer_layer(tokens, weights, seq_first):
    qkv_weight, out_weight, up_weight, down_weight = weights
    model_width = tokens.shape[-1]
    normed = layer_norm(tokens).astype(jnp.bfloat16)
    triple = project(normed, qkv_weight).astype(jnp.bfloat16)
    attended = attend(triple[..., :model_width], triple[..., model_width:2 * model_width], triple[..., 2 * model_width:], seq_first)
    after_attention = rounded(tokens.astype(jnp.float32) + project(attended, out_weight))
    normed_again = layer_norm(after_attention).astype(jnp.bfloat16)
    hidden = jax.nn.relu(project(normed_again, up_weight)).astype(jnp.bfloat16)
    return (after_attention.astype(jnp.float32) + project(hidden, down_weight)).astype(jnp.bfloat16)

def reference(waveform, enc_weight, intra_qkv, intra_out, intra_up, intra_down, inter_qkv, inter_out, inter_up, inter_down, mask_weight):
    blocks = waveform.reshape(FRAMES, HOP)
    following = jnp.concatenate([blocks[1:], jnp.zeros((1, HOP), blocks.dtype)], axis=0)
    framed = jnp.concatenate([blocks, following], axis=1)
    encoded = rounded(jax.nn.relu(jnp.dot(framed, enc_weight, precision=lax.Precision.HIGHEST, preferred_element_type=jnp.float32)))
    padded = jnp.concatenate([encoded, jnp.zeros((HALF, D), jnp.bfloat16)], axis=0)
    padded = padded.reshape(SEGMENTS + 1, HALF, D)
    segmented = jnp.concatenate([padded[:-1], padded[1:]], axis=1)
    intra_weights = (intra_qkv, intra_out, intra_up, intra_down)
    inter_weights = (inter_qkv, inter_out, inter_up, inter_down)

    def within_one(segment_rows):
        return transformer_layer(segment_rows[None], intra_weights, False)[0]
    within = lax.map(within_one, segmented)
    by_position = jnp.swapaxes(within, 0, 1)

    def across_one(position_rows):
        return transformer_layer(position_rows[:, None, :], inter_weights, True)[:, 0, :]
    across = lax.map(across_one, by_position)
    halves = jnp.swapaxes(across, 0, 1).reshape(SEGMENTS, 2, HALF, D)
    lagged = jnp.concatenate([jnp.zeros((1, HALF, D), jnp.bfloat16), halves[:-1, 1]], axis=0)
    combined = rounded(halves[:, 0].astype(jnp.float32) + lagged.astype(jnp.float32)).reshape(FRAMES, D)
    activated = combined.astype(jnp.float32)
    activated = jnp.where(activated > 0, activated, 0.25 * activated).astype(jnp.bfloat16)
    mask_values = jax.nn.relu(jnp.dot(activated, mask_weight, preferred_element_type=jnp.float32))
    mask_values = mask_values.reshape(FRAMES, 2, D)
    separated = (mask_values * encoded.astype(jnp.float32)[:, None, :]).astype(jnp.bfloat16)
    return jnp.transpose(separated, (1, 0, 2))
```

```python
import math

import jax
import jax.numpy as jnp
from jax import lax
from jax.experimental import pallas as pl
from jax.experimental.pallas import tpu as pltpu
from jax.sharding import PartitionSpec as P

HEADS = 8
HEAD = 32
HOP = 8
HALF = 128


def shifted(value, axis, steps):
    count = lax.axis_size(axis)
    leading, last = (max(0, -steps), min(count, count - steps))
    return lax.ppermute(value, axis, [(source, source + steps) for source in range(leading, last)])


def rounded(values):
    return lax.optimization_barrier(values.astype(jnp.bfloat16))


def layer_norm(values):
    values = values.astype(jnp.float32)
    centred = values - jnp.mean(values, axis=-1, keepdims=True)
    spread = jnp.mean(centred * centred, axis=-1, keepdims=True)
    return centred * lax.rsqrt(spread + 1e-05)


def project(values, weight):
    flattened = values.reshape(-1, values.shape[-1])
    result = jnp.dot(flattened, weight, preferred_element_type=jnp.float32)
    return result.reshape(values.shape[:-1] + (weight.shape[1],))


def attend(queries, key_rows, value_rows, seq_first):
    full_shape = queries.shape
    split_shape = full_shape[:-1] + (HEADS, HEAD)
    query_heads = queries.reshape(split_shape)
    key_heads = key_rows.reshape(split_shape)
    value_heads = value_rows.reshape(split_shape)
    if seq_first:
        score_form = "lbhe,kbhe->bhlk"
        weigh_form = "bhlk,kbhe->lbhe"
    else:
        score_form = "blhe,bkhe->bhlk"
        weigh_form = "bhlk,bkhe->blhe"
    scores = jnp.einsum(
        score_form, query_heads, key_heads, preferred_element_type=jnp.float32
    ) * HEAD ** (-0.5)
    probs = jax.nn.softmax(scores, axis=-1).astype(jnp.bfloat16)
    mixture = jnp.einsum(weigh_form, probs, value_heads, preferred_element_type=jnp.float32)
    return mixture.astype(jnp.bfloat16).reshape(full_shape)


def transformer_layer(tokens, weights, seq_first):
    qkv_weight, out_weight, up_weight, down_weight = weights
    model_width = tokens.shape[-1]
    normed = layer_norm(tokens).astype(jnp.bfloat16)
    triple = project(normed, qkv_weight).astype(jnp.bfloat16)
    attended = attend(
        triple[..., :model_width],
        triple[..., model_width : 2 * model_width],
        triple[..., 2 * model_width :],
        seq_first,
    )
    after_attention = rounded(tokens.astype(jnp.float32) + project(attended, out_weight))
    normed_again = layer_norm(after_attention).astype(jnp.bfloat16)
    hidden = jax.nn.relu(project(normed_again, up_weight)).astype(jnp.bfloat16)
    return (after_attention.astype(jnp.float32) + project(hidden, down_weight)).astype(jnp.bfloat16)


def encode(framed, enc_weight):
    return rounded(
        jax.nn.relu(
            jnp.dot(
                framed,
                enc_weight,
                precision=lax.Precision.HIGHEST,
                preferred_element_type=jnp.float32,
            )
        )
    )


def local(
    waveform,
    enc_weight,
    intra_qkv,
    intra_out,
    intra_up,
    intra_down,
    inter_qkv,
    inter_out,
    inter_up,
    inter_down,
    mask_weight,
):
    model_width = enc_weight.shape[1]
    frames_here = waveform.shape[0] // HOP
    blocks = waveform.reshape(frames_here, HOP)
    first_block = shifted(blocks[:1], "tm", -1)
    following = jnp.concatenate([blocks[1:], first_block], axis=0)
    framed = jnp.concatenate([blocks, following], axis=1)
    encoded = encode(framed, enc_weight)
    frame_edge = shifted(encoded[:HALF], "tm", -1)
    padded = jnp.concatenate([encoded, frame_edge], axis=0)
    segment_total = frames_here // HALF
    stacked = padded.reshape(segment_total + 1, HALF, model_width)
    segmented = jnp.concatenate([stacked[:-1], stacked[1:]], axis=1)
    intra_weights = (intra_qkv, intra_out, intra_up, intra_down)
    inter_weights = (inter_qkv, inter_out, inter_up, inter_down)
    within = transformer_layer(segmented, intra_weights, False)
    within = within.reshape(segment_total, 2, HALF, model_width)
    pieces = lax.all_to_all(within, "tm", split_axis=2, concat_axis=0, tiled=True)
    row_total, item_count, spot_count, feature_count = pieces.shape
    flattened = pieces.reshape(row_total, item_count * spot_count, feature_count)
    result = transformer_layer(flattened, inter_weights, True)
    across = result.reshape(row_total, item_count, spot_count, feature_count)
    returned = lax.all_to_all(across, "tm", split_axis=0, concat_axis=2, tiled=True)
    tail_half = shifted(returned[-1:, 1], "tm", 1)
    lagged = jnp.concatenate([tail_half, returned[:-1, 1]], axis=0)
    combined = rounded(returned[:, 0].astype(jnp.float32) + lagged.astype(jnp.float32))
    combined = combined.reshape(frames_here, model_width)
    activated = combined.astype(jnp.float32)
    activated = jnp.where(activated > 0, activated, 0.25 * activated).astype(jnp.bfloat16)
    mask_values = jax.nn.relu(jnp.dot(activated, mask_weight, preferred_element_type=jnp.float32))
    mask_values = mask_values.reshape(frames_here, 2, model_width)
    separated = (mask_values * encoded.astype(jnp.float32)[:, None, :]).astype(jnp.bfloat16)
    return jnp.transpose(separated, (1, 0, 2))


def split_three(values):
    high = values.astype(jnp.bfloat16)
    rest = values - high.astype(jnp.float32)
    middle = rest.astype(jnp.bfloat16)
    low = (rest - middle.astype(jnp.float32)).astype(jnp.bfloat16)
    return high, middle, low


def normalise(values):
    centred = values - jnp.mean(values, axis=-1, keepdims=True)
    spread = jnp.mean(centred * centred, axis=-1, keepdims=True)
    return (centred * lax.rsqrt(spread + 1e-05)).astype(jnp.bfloat16)


def dot(left, right):
    return jnp.dot(left, right, preferred_element_type=jnp.float32)


def dot_nt(left, right):
    return lax.dot_general(left, right, (((1,), (1,)), ((), ())), preferred_element_type=jnp.float32)


def head_of(shape, axis):
    return lax.broadcasted_iota(jnp.int32, shape, axis) // HEAD


def by_head(queries):
    lanes = head_of(queries.shape, 1)
    zero = jnp.zeros_like(queries)
    return jnp.concatenate([jnp.where(lanes == h, queries, zero) for h in range(HEADS)], axis=0)


def feed_forward(tokens, attended, out_ref, up_ref, down_ref):
    after = (tokens + dot(attended, out_ref[...])).astype(jnp.bfloat16).astype(jnp.float32)
    hidden = jnp.maximum(dot(normalise(after), up_ref[...]), 0.0).astype(jnp.bfloat16)
    return (after + dot(hidden, down_ref[...])).astype(jnp.bfloat16).astype(jnp.float32)


SCORE_SCALE = math.log2(math.e) * HEAD ** (-0.5)
GROUP = 16


def encode_chunk(c, chunks, wave_ref, stacked_weight, enc_ref, normed_ref):
    taps = wave_ref[c]
    count = taps.shape[1]
    following = wave_ref[jnp.minimum(c + 1, chunks - 1)]
    lanes = lax.broadcasted_iota(jnp.int32, taps.shape, 1)
    edge = jnp.where(c + 1 < chunks, pltpu.roll(following, count - 1, 1), 0.0)
    shifted_taps = jnp.where(lanes < count - 1, pltpu.roll(taps, count - 1, 1), edge)
    high, middle, low = split_three(jnp.concatenate([taps, shifted_taps], axis=0))
    pad = jnp.zeros((32, count), jnp.bfloat16)
    stacked = jnp.concatenate([high, high, middle, high, low, middle, pad], axis=0)
    rows = count // 4
    for part in range(4):
        piece = stacked[:, part * rows : (part + 1) * rows]
        frames = lax.dot_general(
            piece, stacked_weight, (((0,), (0,)), ((), ())), preferred_element_type=jnp.float32
        )
        encoded = jnp.maximum(frames, 0.0).astype(jnp.bfloat16)
        at = pl.ds(pl.multiple_of(c * count + part * rows, rows), rows)
        enc_ref[at, :] = encoded
        normed_ref[at, :] = normalise(encoded.astype(jnp.float32))


def stack_weight(weight):
    high, middle, low = split_three(weight)
    pad = jnp.zeros((32, weight.shape[1]), jnp.bfloat16)
    return jnp.concatenate([high, middle, high, low, high, middle, pad], axis=0)


def intra_group(g, place, enc_ref, normed_ref, u_ref, pn_ref, key_ref, value_ref, within_ref, qkv_ref, out_ref, up_ref, down_ref):
    width = enc_ref.shape[1]
    start = pl.multiple_of(16 * (place // 2), 16)
    odd = place % 2 == 1
    picked = []
    for b in range(GROUP + 1):
        rows = enc_ref[pl.ds(pl.multiple_of((GROUP * g + b) * HALF + start, 16), 16), :].astype(jnp.float32)
        picked.append(jnp.where(odd, rows[8:], rows[:8]))
    tokens = jnp.concatenate(
        [half for b in range(GROUP) for half in (picked[b], picked[b + 1])], axis=0
    )
    queries = (dot(normalise(tokens), qkv_ref[:, :width]) * SCORE_SCALE).astype(jnp.bfloat16)
    lanes = head_of(queries.shape, 1)
    for h in range(HEADS):
        own = jnp.where(lanes == h, queries, jnp.zeros_like(queries))
        u_ref[h] = dot(own, key_ref[...]).astype(jnp.bfloat16)
    for s in range(GROUP):
        at = slice(16 * s, 16 * s + 16)
        u = u_ref[:, at, :].reshape(16 * HEADS, width)
        keys = normed_ref[pl.ds(pl.multiple_of((GROUP * g + s) * HALF, HALF), 2 * HALF), :]
        scores = dot_nt(u, keys)
        probs = jnp.exp2(scores - jnp.max(scores, axis=-1, keepdims=True))
        total = jnp.sum(probs, axis=-1, keepdims=True)
        mixed = dot(probs.astype(jnp.bfloat16), keys) * (1.0 / total)
        pn_ref[:, at, :] = mixed.astype(jnp.bfloat16).reshape(HEADS, 16, width)
    attended = dot(pn_ref[0], value_ref[0])
    for h in range(1, HEADS):
        attended += dot(pn_ref[h], value_ref[h])
    result = feed_forward(tokens, attended.astype(jnp.bfloat16), out_ref, up_ref, down_ref)
    for part in range(width // 128):
        within_ref[part, pl.ds(pl.multiple_of(g * GROUP * 16, GROUP * 16), GROUP * 16), :] = result[
            :, part * 128 : part * 128 + 128
        ]


def inter_spot(s, segments, within_ref, qkv_ref, out_ref, up_ref, down_ref):
    width = qkv_ref.shape[0]
    tokens = jnp.concatenate(
        [
            jnp.concatenate(
                [within_ref.at[part][pl.ds(s + 8 * half, segments, stride=16), :] for part in range(width // 128)],
                axis=1,
            )
            for half in range(2)
        ],
        axis=0,
    )
    triple = dot(normalise(tokens), qkv_ref[...])
    queries = (triple[:, :width] * SCORE_SCALE).astype(jnp.bfloat16)
    keys = triple[:, width : 2 * width].astype(jnp.bfloat16)
    values = triple[:, 2 * width :].astype(jnp.bfloat16)
    lanes = head_of((segments, width), 1)
    parts = []
    for half in range(2):
        at = slice(half * segments, (half + 1) * segments)
        scores = dot_nt(by_head(queries[at]), keys[at])
        probs = jnp.exp2(scores - jnp.max(scores, axis=-1, keepdims=True))
        total = jnp.sum(probs, axis=-1, keepdims=True)
        mixed = dot(probs.astype(jnp.bfloat16), values[at])
        inverse = 1.0 / total
        attended = jnp.zeros((segments, width), jnp.float32)
        for h in range(HEADS):
            rows = slice(h * segments, (h + 1) * segments)
            attended = jnp.where(lanes == h, mixed[rows] * inverse[rows], attended)
        parts.append(attended.astype(jnp.bfloat16))
    across = feed_forward(tokens, jnp.concatenate(parts, axis=0), out_ref, up_ref, down_ref)
    first, second = across[:segments], across[segments:]
    row = lax.broadcasted_iota(jnp.int32, second.shape, 0)
    lagged = jnp.where(row == 0, 0.0, pltpu.roll(second, 1, 0))
    combined = (first + lagged).astype(jnp.bfloat16).astype(jnp.float32)
    return jnp.where(combined > 0, combined, 0.25 * combined).astype(jnp.bfloat16)


def prepare(wave_ref, normed_ref, enc_ref, key_ref, value_ref, qkv_ref):
    width = qkv_ref.shape[0]
    tail = normed_ref.shape[0] - HALF
    normed_ref[tail:, :] = jnp.zeros((HALF, width), jnp.bfloat16)
    enc_ref[tail:, :] = jnp.zeros((HALF, width), jnp.bfloat16)
    key_ref[...] = qkv_ref[:, width : 2 * width].astype(jnp.float32).T.astype(jnp.bfloat16)
    values = qkv_ref[:, 2 * width :]
    lanes = head_of(values.shape, 1)
    for h in range(HEADS):
        value_ref[h] = jnp.where(lanes == h, values, jnp.zeros_like(values))


def layers_kernel(
    wave_ref, enc_weight_ref,
    qkv_ref, out_ref, up_ref, down_ref,
    inter_qkv_ref, inter_out_ref, inter_up_ref, inter_down_ref,
    active_ref, own_ref,
    enc_ref, normed_ref, u_ref, pn_ref, key_ref, value_ref, within_ref,
):
    place = lax.axis_index("tm")
    chunks, _, count = wave_ref.shape
    segments = active_ref.shape[1]
    prepare(wave_ref, normed_ref, enc_ref, key_ref, value_ref, qkv_ref)
    stacked_weight = stack_weight(enc_weight_ref[...])

    @pl.loop(0, chunks)
    def _(c):
        encode_chunk(c, chunks, wave_ref, stacked_weight, enc_ref, normed_ref)

    own_ref[...] = enc_ref[pl.ds(pl.multiple_of(place * count, count), count), :]

    @pl.loop(0, segments // GROUP)
    def _(g):
        intra_group(g, place, enc_ref, normed_ref, u_ref, pn_ref, key_ref, value_ref, within_ref, qkv_ref, out_ref, up_ref, down_ref)

    @pl.loop(0, active_ref.shape[0])
    def _(s):
        active_ref[s] = inter_spot(
            s, segments, within_ref, inter_qkv_ref, inter_out_ref, inter_up_ref, inter_down_ref
        )


def local_positions(
    waveform, enc_weight, intra_qkv, intra_out, intra_up, intra_down,
    inter_qkv, inter_out, inter_up, inter_down, mask_weight,
):
    width = enc_weight.shape[1]
    devices = lax.axis_size("tm")
    here = waveform.shape[0] // HOP
    frames = here * devices
    segments = frames // HALF
    spots = HALF // devices
    taps = waveform.reshape(here, HOP).T
    wave = lax.all_gather(taps, "tm")
    vmem = pl.BlockSpec(memory_space=pltpu.VMEM)
    active, encoded = pl.pallas_call(
        layers_kernel,
        out_shape=(
            jax.ShapeDtypeStruct((spots, segments, width), jnp.bfloat16),
            jax.ShapeDtypeStruct((here, width), jnp.bfloat16),
        ),
        in_specs=[vmem] * 10,
        out_specs=(vmem, vmem),
        scratch_shapes=[
            pltpu.VMEM((frames + HALF, width), jnp.bfloat16),
            pltpu.VMEM((frames + HALF, width), jnp.bfloat16),
            pltpu.VMEM((HEADS, GROUP * 16, width), jnp.bfloat16),
            pltpu.VMEM((HEADS, GROUP * 16, width), jnp.bfloat16),
            pltpu.VMEM((width, width), jnp.bfloat16),
            pltpu.VMEM((HEADS, width, width), jnp.bfloat16),
            pltpu.VMEM((width // 128, segments * 16, 128), jnp.float32),
        ],
        compiler_params=pltpu.CompilerParams(vmem_limit_bytes=56 * 1024 * 1024),
        name="layers",
    )(wave, enc_weight, intra_qkv, intra_out, intra_up, intra_down, inter_qkv, inter_out, inter_up, inter_down)
    pieces = lax.all_to_all(
        active.reshape(spots, devices, segments // devices, width), "tm", split_axis=1, concat_axis=0, tiled=True
    )
    activated = pieces.reshape(HALF, segments // devices, width).transpose(1, 0, 2).reshape(here, width)
    mask_values = jax.nn.relu(jnp.dot(activated, mask_weight, preferred_element_type=jnp.float32))
    mask_values = mask_values.reshape(here, 2, width)
    separated = (mask_values * encoded.astype(jnp.float32)[:, None, :]).astype(jnp.bfloat16)
    return jnp.transpose(separated, (1, 0, 2))


def solution(mesh):
    body = local_positions if mesh.shape["tm"] * 8 == HALF else local
    return jax.shard_map(
        body,
        mesh=mesh,
        in_specs=(P(("grp", "tm")), P(), P(), P(), P(), P(), P(), P(), P(), P(), P()),
        out_specs=P(None, ("grp", "tm"), None),
        check_vma=False,
    )
```

```python
import functools
import math

import jax
import jax.numpy as jnp
from jax import lax
from jax.experimental import pallas as pl
from jax.experimental.pallas import tpu as pltpu
from jax.sharding import PartitionSpec as P

HEADS = 8
HEAD = 32
HOP = 8
HALF = 128


def shifted(value, axis, steps):
    count = lax.axis_size(axis)
    leading, last = (max(0, -steps), min(count, count - steps))
    return lax.ppermute(value, axis, [(source, source + steps) for source in range(leading, last)])


def rounded(values):
    return lax.optimization_barrier(values.astype(jnp.bfloat16))


def layer_norm(values):
    values = values.astype(jnp.float32)
    centred = values - jnp.mean(values, axis=-1, keepdims=True)
    spread = jnp.mean(centred * centred, axis=-1, keepdims=True)
    return centred * lax.rsqrt(spread + 1e-05)


def project(values, weight):
    flattened = values.reshape(-1, values.shape[-1])
    result = jnp.dot(flattened, weight, preferred_element_type=jnp.float32)
    return result.reshape(values.shape[:-1] + (weight.shape[1],))


def attend(queries, key_rows, value_rows, seq_first):
    full_shape = queries.shape
    split_shape = full_shape[:-1] + (HEADS, HEAD)
    query_heads = queries.reshape(split_shape)
    key_heads = key_rows.reshape(split_shape)
    value_heads = value_rows.reshape(split_shape)
    if seq_first:
        score_form = "lbhe,kbhe->bhlk"
        weigh_form = "bhlk,kbhe->lbhe"
    else:
        score_form = "blhe,bkhe->bhlk"
        weigh_form = "bhlk,bkhe->blhe"
    scores = jnp.einsum(
        score_form, query_heads, key_heads, preferred_element_type=jnp.float32
    ) * HEAD ** (-0.5)
    probs = jax.nn.softmax(scores, axis=-1).astype(jnp.bfloat16)
    mixture = jnp.einsum(weigh_form, probs, value_heads, preferred_element_type=jnp.float32)
    return mixture.astype(jnp.bfloat16).reshape(full_shape)


def transformer_layer(tokens, weights, seq_first):
    qkv_weight, out_weight, up_weight, down_weight = weights
    model_width = tokens.shape[-1]
    normed = layer_norm(tokens).astype(jnp.bfloat16)
    triple = project(normed, qkv_weight).astype(jnp.bfloat16)
    attended = attend(
        triple[..., :model_width],
        triple[..., model_width : 2 * model_width],
        triple[..., 2 * model_width :],
        seq_first,
    )
    after_attention = rounded(tokens.astype(jnp.float32) + project(attended, out_weight))
    normed_again = layer_norm(after_attention).astype(jnp.bfloat16)
    hidden = jax.nn.relu(project(normed_again, up_weight)).astype(jnp.bfloat16)
    return (after_attention.astype(jnp.float32) + project(hidden, down_weight)).astype(jnp.bfloat16)


def encode(framed, enc_weight):
    return rounded(
        jax.nn.relu(
            jnp.dot(
                framed,
                enc_weight,
                precision=lax.Precision.HIGHEST,
                preferred_element_type=jnp.float32,
            )
        )
    )


def local(
    waveform,
    enc_weight,
    intra_qkv,
    intra_out,
    intra_up,
    intra_down,
    inter_qkv,
    inter_out,
    inter_up,
    inter_down,
    mask_weight,
):
    model_width = enc_weight.shape[1]
    frames_here = waveform.shape[0] // HOP
    blocks = waveform.reshape(frames_here, HOP)
    first_block = shifted(blocks[:1], "tm", -1)
    following = jnp.concatenate([blocks[1:], first_block], axis=0)
    framed = jnp.concatenate([blocks, following], axis=1)
    encoded = encode(framed, enc_weight)
    frame_edge = shifted(encoded[:HALF], "tm", -1)
    padded = jnp.concatenate([encoded, frame_edge], axis=0)
    segment_total = frames_here // HALF
    stacked = padded.reshape(segment_total + 1, HALF, model_width)
    segmented = jnp.concatenate([stacked[:-1], stacked[1:]], axis=1)
    intra_weights = (intra_qkv, intra_out, intra_up, intra_down)
    inter_weights = (inter_qkv, inter_out, inter_up, inter_down)
    within = transformer_layer(segmented, intra_weights, False)
    within = within.reshape(segment_total, 2, HALF, model_width)
    pieces = lax.all_to_all(within, "tm", split_axis=2, concat_axis=0, tiled=True)
    row_total, item_count, spot_count, feature_count = pieces.shape
    flattened = pieces.reshape(row_total, item_count * spot_count, feature_count)
    result = transformer_layer(flattened, inter_weights, True)
    across = result.reshape(row_total, item_count, spot_count, feature_count)
    returned = lax.all_to_all(across, "tm", split_axis=0, concat_axis=2, tiled=True)
    tail_half = shifted(returned[-1:, 1], "tm", 1)
    lagged = jnp.concatenate([tail_half, returned[:-1, 1]], axis=0)
    combined = rounded(returned[:, 0].astype(jnp.float32) + lagged.astype(jnp.float32))
    combined = combined.reshape(frames_here, model_width)
    activated = combined.astype(jnp.float32)
    activated = jnp.where(activated > 0, activated, 0.25 * activated).astype(jnp.bfloat16)
    mask_values = jax.nn.relu(jnp.dot(activated, mask_weight, preferred_element_type=jnp.float32))
    mask_values = mask_values.reshape(frames_here, 2, model_width)
    separated = (mask_values * encoded.astype(jnp.float32)[:, None, :]).astype(jnp.bfloat16)
    return jnp.transpose(separated, (1, 0, 2))


def split_three(values):
    high = values.astype(jnp.bfloat16)
    rest = values - high.astype(jnp.float32)
    middle = rest.astype(jnp.bfloat16)
    low = (rest - middle.astype(jnp.float32)).astype(jnp.bfloat16)
    return high, middle, low


def normalise(values):
    centred = values - jnp.mean(values, axis=-1, keepdims=True)
    spread = jnp.mean(centred * centred, axis=-1, keepdims=True)
    return (centred * lax.rsqrt(spread + 1e-05)).astype(jnp.bfloat16)


def dot(left, right):
    return jnp.dot(left, right, preferred_element_type=jnp.float32)


def dot_nt(left, right):
    return lax.dot_general(left, right, (((1,), (1,)), ((), ())), preferred_element_type=jnp.float32)


def head_of(shape, axis):
    return lax.broadcasted_iota(jnp.int32, shape, axis) // HEAD


def by_head(queries):
    lanes = head_of(queries.shape, 1)
    zero = jnp.zeros_like(queries)
    return [jnp.where(lanes == h, queries, zero) for h in range(queries.shape[1] // HEAD)]


def feed_forward(tokens, attended, out_ref, up_ref, down_ref):
    after = (tokens + dot(attended, out_ref[...])).astype(jnp.bfloat16).astype(jnp.float32)
    hidden = jnp.maximum(dot(normalise(after), up_ref[...]), 0.0).astype(jnp.bfloat16)
    return (after + dot(hidden, down_ref[...])).astype(jnp.bfloat16).astype(jnp.float32)


SCORE_SCALE = math.log2(math.e) * HEAD ** (-0.5)
GROUP = 32
BATCH = 8
LANES = 128
NEAR = LANES // HEAD


def encode_chunk(c, wave_ref, stacked_weight, enc_ref, normed_ref):
    taps = wave_ref[c]
    count = taps.shape[1] - LANES
    following = pltpu.roll(taps, taps.shape[1] - 1, 1)
    high, middle, low = split_three(jnp.concatenate([taps[:, :count], following[:, :count]], axis=0))
    pad = jnp.zeros((32, count), jnp.bfloat16)
    stacked = jnp.concatenate([high, high, middle, high, low, middle, pad], axis=0)
    rows = count // 4
    for part in range(4):
        piece = stacked[:, part * rows : (part + 1) * rows]
        frames = lax.dot_general(
            piece, stacked_weight, (((0,), (0,)), ((), ())), preferred_element_type=jnp.float32
        )
        encoded = jnp.maximum(frames, 0.0).astype(jnp.bfloat16)
        at = pl.ds(pl.multiple_of(c * count + part * rows, rows), rows)
        enc_ref[at, :] = encoded
        normed_ref[at, :] = normalise(encoded.astype(jnp.float32))


def stack_weight(weight):
    high, middle, low = split_three(weight)
    pad = jnp.zeros((32, weight.shape[1]), jnp.bfloat16)
    return jnp.concatenate([high, middle, high, low, high, middle, pad], axis=0)


def intra_group(g, place, enc_ref, normed_ref, u_ref, pn_ref, key_ref, value_ref, within_ref, qkv_ref, out_ref, up_ref, down_ref):
    width = enc_ref.shape[1]
    start = pl.multiple_of(16 * (place // 2), 16)
    odd = place % 2 == 1
    picked = []
    for b in range(GROUP + 1):
        rows = enc_ref[pl.ds(pl.multiple_of((GROUP * g + b) * HALF + start, 16), 16), :].astype(jnp.float32)
        picked.append(jnp.where(odd, rows[8:], rows[:8]))
    tokens = jnp.concatenate(
        [half for b in range(GROUP) for half in (picked[b], picked[b + 1])], axis=0
    )
    queries = (dot(normalise(tokens), qkv_ref[:, :width]) * SCORE_SCALE).astype(jnp.bfloat16)
    for part in range(width // LANES):
        at = slice(part * LANES, (part + 1) * LANES)
        for h, own in enumerate(by_head(queries[:, at])):
            u_ref[part * NEAR + h] = dot(own, key_ref[at, :]).astype(jnp.bfloat16)

    @pl.loop(0, GROUP // BATCH)
    def _(i):
        spans = [pl.ds(pl.multiple_of((i * BATCH + s) * 16, 16), 16) for s in range(BATCH)]
        spots = [
            pl.ds(pl.multiple_of((GROUP * g + i * BATCH + s) * HALF, HALF), 2 * HALF) for s in range(BATCH)
        ]
        scores = [
            dot_nt(u_ref[:, spans[s], :].reshape(16 * HEADS, width), normed_ref[spots[s], :])
            for s in range(BATCH)
        ]
        tops = [jnp.max(each, axis=-1, keepdims=True) for each in scores]
        probs = [jnp.exp2(each - top) for each, top in zip(scores, tops)]
        totals = [jnp.sum(each, axis=-1, keepdims=True) for each in probs]
        mixed = [dot(probs[s].astype(jnp.bfloat16), normed_ref[spots[s], :]) for s in range(BATCH)]
        for s in range(BATCH):
            scaled = mixed[s] * (1.0 / totals[s])
            pn_ref[:, spans[s], :] = scaled.astype(jnp.bfloat16).reshape(HEADS, 16, width)

    sides = []
    for part in range(width // LANES):
        side = dot(pn_ref[part * NEAR], value_ref[part * NEAR])
        for h in range(part * NEAR + 1, (part + 1) * NEAR):
            side += dot(pn_ref[h], value_ref[h])
        sides.append(side.astype(jnp.bfloat16))
    result = feed_forward(tokens, jnp.concatenate(sides, axis=1), out_ref, up_ref, down_ref)
    at = pl.ds(pl.multiple_of(g * GROUP * 16, GROUP * 16), GROUP * 16)
    for part in range(width // LANES):
        within_ref[part, at, :] = result[:, part * LANES : (part + 1) * LANES]


def inter_pair(t, segments, within_ref, qkv_ref, out_ref, up_ref, down_ref):
    width = qkv_ref.shape[0]
    sides = range(width // LANES)
    places = [(spot, half) for spot in range(2) for half in range(2)]
    tokens = jnp.concatenate(
        [
            jnp.concatenate(
                [
                    within_ref.at[part][pl.ds(2 * t + spot + 8 * half, segments, stride=16), :]
                    for part in sides
                ],
                axis=1,
            )
            for spot, half in places
        ],
        axis=0,
    )
    triple = dot(normalise(tokens), qkv_ref[...])
    queries = (triple[:, :width] * SCORE_SCALE).astype(jnp.bfloat16)
    keys = triple[:, width : 2 * width].astype(jnp.bfloat16)
    values = triple[:, 2 * width :].astype(jnp.bfloat16)
    lanes = head_of((segments, LANES), 1)
    columns = []
    for part in sides:
        wide = slice(part * LANES, (part + 1) * LANES)
        rows = [slice(p * segments, (p + 1) * segments) for p in range(len(places))]
        scores = [
            dot_nt(jnp.concatenate(by_head(queries[at, wide]), axis=0), keys[at, wide]) for at in rows
        ]
        probs = [jnp.exp2(each - jnp.max(each, axis=-1, keepdims=True)) for each in scores]
        probs = [
            (each * (1.0 / jnp.sum(each, axis=-1, keepdims=True))).astype(jnp.bfloat16) for each in probs
        ]
        mixed = [dot(each, values[at, wide]) for each, at in zip(probs, rows)]
        parts = []
        for each in mixed:
            attended = each[:segments]
            for h in range(1, NEAR):
                attended = jnp.where(lanes == h, each[h * segments : (h + 1) * segments], attended)
            parts.append(attended.astype(jnp.bfloat16))
        columns.append(jnp.concatenate(parts, axis=0))
    across = feed_forward(tokens, jnp.concatenate(columns, axis=1), out_ref, up_ref, down_ref)
    row = lax.broadcasted_iota(jnp.int32, (segments, width), 0)
    results = []
    for spot in range(2):
        first = across[2 * spot * segments : (2 * spot + 1) * segments]
        second = across[(2 * spot + 1) * segments : (2 * spot + 2) * segments]
        lagged = jnp.where(row == 0, 0.0, pltpu.roll(second, 1, 0))
        combined = (first + lagged).astype(jnp.bfloat16).astype(jnp.float32)
        results.append(jnp.where(combined > 0, combined, 0.25 * combined))
    return results


def prepare(normed_ref, enc_ref, key_ref, value_ref, qkv_ref):
    width = qkv_ref.shape[0]
    tail = normed_ref.shape[0] - HALF
    normed_ref[tail:, :] = jnp.zeros((HALF, width), jnp.bfloat16)
    enc_ref[tail:, :] = jnp.zeros((HALF, width), jnp.bfloat16)
    key_ref[...] = qkv_ref[:, width : 2 * width].astype(jnp.float32).T.astype(jnp.bfloat16)
    for part in range(width // LANES):
        start = 2 * width + part * LANES
        for h, own in enumerate(by_head(qkv_ref[:, start : start + LANES])):
            value_ref[part * NEAR + h] = own


def layers_kernel(
    devices,
    taps_ref, enc_weight_ref,
    qkv_ref, out_ref, up_ref, down_ref,
    inter_qkv_ref, inter_out_ref, inter_up_ref, inter_down_ref,
    active_ref, own_ref,
    wave_ref, halo_ref, enc_ref, normed_ref, u_ref, pn_ref, key_ref, value_ref, within_ref,
    send_ref, landed_ref,
    halo_sems, wave_sent, wave_landed, rows_sent, rows_landed,
):
    place = lax.axis_index("tm")
    count, width = own_ref.shape
    segments = devices * count // HALF
    stages = send_ref.shape[0]
    blocks = count // HALF

    def peer(k, sign):
        far = (place // 4 + sign * (k // 4) + devices) % (devices // 4)
        return far * 4 + (place // 2 + k // 2) % 2 * 2 + (place + k) % 2

    barrier = pltpu.get_barrier_semaphore()

    @pl.loop(1, devices)
    def _(k):
        pl.semaphore_signal(barrier, inc=1, device_id={"tm": peer(k, 1)}, device_id_type=pl.DeviceIdType.MESH)

    pl.semaphore_wait(barrier, devices - 1)
    halo = pltpu.make_async_remote_copy(
        src_ref=taps_ref.at[:, pl.ds(0, LANES)],
        dst_ref=halo_ref,
        send_sem=halo_sems.at[0],
        recv_sem=halo_sems.at[1],
        device_id={"tm": (place + devices - 1) % devices},
        device_id_type=pl.DeviceIdType.MESH,
    )
    halo.start()
    prepare(normed_ref, enc_ref, key_ref, value_ref, qkv_ref)
    stacked_weight = stack_weight(enc_weight_ref[...])
    wave_ref[place, :, :count] = taps_ref[...]
    halo.wait()
    wave_ref[place, :, count:] = jnp.where(place < devices - 1, halo_ref[...], 0.0)

    def wave_copy(k, slot):
        return pltpu.make_async_remote_copy(
            src_ref=wave_ref.at[slot],
            dst_ref=wave_ref.at[slot],
            send_sem=wave_sent.at[k],
            recv_sem=wave_landed.at[k],
            device_id={"tm": peer(k, 1)},
            device_id_type=pl.DeviceIdType.MESH,
        )

    @pl.loop(1, devices)
    def _(k):
        wave_copy(k, place).start()

    encode_chunk(place, wave_ref, stacked_weight, enc_ref, normed_ref)
    own_ref[...] = enc_ref[pl.ds(pl.multiple_of(place * count, count), count), :]

    @pl.loop(1, devices)
    def _(k):
        source = peer(k, -1)
        wave_copy(k, source).wait_recv()
        encode_chunk(source, wave_ref, stacked_weight, enc_ref, normed_ref)

    @pl.loop(1, devices)
    def _(k):
        wave_copy(k, place).wait_send()

    @pl.loop(0, segments // GROUP)
    def _(g):
        intra_group(g, place, enc_ref, normed_ref, u_ref, pn_ref, key_ref, value_ref, within_ref, qkv_ref, out_ref, up_ref, down_ref)

    def rows_copy(t, k, slot):
        return pltpu.make_async_remote_copy(
            src_ref=send_ref.at[t, peer(k, 1)],
            dst_ref=landed_ref.at[slot, t],
            send_sem=rows_sent.at[t, k],
            recv_sem=rows_landed.at[t, k],
            device_id={"tm": peer(k, 1)},
            device_id_type=pl.DeviceIdType.MESH,
        )

    @pl.loop(0, stages)
    def _(t):
        pair = inter_pair(t, segments, within_ref, inter_qkv_ref, inter_out_ref, inter_up_ref, inter_down_ref)
        pair = [each.reshape(devices, blocks, width) for each in pair]
        send_ref[t] = jnp.concatenate(pair, axis=1).astype(jnp.bfloat16)
        landed_ref[place, t] = send_ref[t, place]

        @pl.loop(1, devices)
        def _(k):
            rows_copy(t, devices - k, place).start()

    @pl.loop(0, stages)
    def _(t):
        @pl.loop(1, devices)
        def _(k):
            rows_copy(t, k, peer(k, -1)).wait_recv()

    for source in range(devices):
        for t in range(stages):
            rows = landed_ref[source, t].astype(jnp.float32)
            for spot in range(2):
                for part in range(width // LANES):
                    at = pl.ds(2 * stages * source + 2 * t + spot, blocks, stride=HALF)
                    within_ref.at[part][at, :] = rows[
                        spot * blocks : (spot + 1) * blocks, part * LANES : (part + 1) * LANES
                    ]
    for part in range(width // LANES):
        active_ref[:, part * LANES : (part + 1) * LANES] = within_ref[part, :count, :].astype(jnp.bfloat16)

    @pl.loop(0, stages)
    def _(t):
        @pl.loop(1, devices)
        def _(k):
            rows_copy(t, k, place).wait_send()


def mask_kernel(active_ref, encoded_ref, mask_ref, result_ref):
    rows, width = encoded_ref.shape
    step = rows // 4
    for part in range(4):
        at = slice(part * step, (part + 1) * step)
        encoded = encoded_ref[at, :].astype(jnp.float32)
        for speaker in range(2):
            values = dot(active_ref[at, :], mask_ref[:, speaker * width : (speaker + 1) * width])
            result_ref[speaker, at, :] = (jnp.maximum(values, 0.0) * encoded).astype(jnp.bfloat16)


def local_positions(
    waveform, enc_weight, intra_qkv, intra_out, intra_up, intra_down,
    inter_qkv, inter_out, inter_up, inter_down, mask_weight,
):
    width = enc_weight.shape[1]
    devices = lax.axis_size("tm")
    here = waveform.shape[0] // HOP
    frames = here * devices
    segments = frames // HALF
    stages = HALF // devices // 2
    blocks = here // HALF
    taps = waveform.reshape(here, HOP).T
    vmem = pl.BlockSpec(memory_space=pltpu.VMEM)
    half = jnp.bfloat16
    active, encoded = pl.pallas_call(
        functools.partial(layers_kernel, devices),
        out_shape=(jax.ShapeDtypeStruct((here, width), half), jax.ShapeDtypeStruct((here, width), half)),
        in_specs=[vmem] * 10,
        out_specs=(vmem, vmem),
        scratch_shapes=[
            pltpu.VMEM((devices, HOP, here + LANES), jnp.float32),
            pltpu.VMEM((HOP, LANES), jnp.float32),
            pltpu.VMEM((frames + HALF, width), half),
            pltpu.VMEM((frames + HALF, width), half),
            pltpu.VMEM((HEADS, GROUP * 16, width), half),
            pltpu.VMEM((HEADS, GROUP * 16, width), half),
            pltpu.VMEM((width, width), half),
            pltpu.VMEM((HEADS, width, LANES), half),
            pltpu.VMEM((width // LANES, segments * 16, LANES), jnp.float32),
            pltpu.VMEM((stages, devices, 2 * blocks, width), half),
            pltpu.VMEM((devices, stages, 2 * blocks, width), half),
            pltpu.SemaphoreType.DMA((2,)),
            pltpu.SemaphoreType.DMA((devices,)),
            pltpu.SemaphoreType.DMA((devices,)),
            pltpu.SemaphoreType.DMA((stages, devices)),
            pltpu.SemaphoreType.DMA((stages, devices)),
        ],
        compiler_params=pltpu.CompilerParams(
            vmem_limit_bytes=56 * 1024 * 1024, collective_id=0, has_side_effects=True
        ),
        name="layers",
    )(taps, enc_weight, intra_qkv, intra_out, intra_up, intra_down, inter_qkv, inter_out, inter_up, inter_down)
    return pl.pallas_call(
        mask_kernel,
        out_shape=jax.ShapeDtypeStruct((2, here, width), half),
        in_specs=[vmem] * 3,
        out_specs=vmem,
        compiler_params=pltpu.CompilerParams(vmem_limit_bytes=24 * 1024 * 1024),
        name="mask",
    )(active, encoded, mask_weight)


def solution(mesh):
    body = local_positions if mesh.shape["tm"] * 8 == HALF else local
    return jax.shard_map(
        body,
        mesh=mesh,
        in_specs=(P(("grp", "tm")), P(), P(), P(), P(), P(), P(), P(), P(), P(), P()),
        out_specs=P(None, ("grp", "tm"), None),
        check_vma=False,
    )
```

```python
import functools
import math

import jax
import jax.numpy as jnp
from jax import lax
from jax.experimental import pallas as pl
from jax.experimental.pallas import tpu as pltpu
from jax.sharding import PartitionSpec as P

HEADS = 8
HEAD = 32
HOP = 8
HALF = 128


def shifted(value, axis, steps):
    count = lax.axis_size(axis)
    leading, last = (max(0, -steps), min(count, count - steps))
    return lax.ppermute(value, axis, [(source, source + steps) for source in range(leading, last)])


def rounded(values):
    return lax.optimization_barrier(values.astype(jnp.bfloat16))


def layer_norm(values):
    values = values.astype(jnp.float32)
    centred = values - jnp.mean(values, axis=-1, keepdims=True)
    spread = jnp.mean(centred * centred, axis=-1, keepdims=True)
    return centred * lax.rsqrt(spread + 1e-05)


def project(values, weight):
    flattened = values.reshape(-1, values.shape[-1])
    result = jnp.dot(flattened, weight, preferred_element_type=jnp.float32)
    return result.reshape(values.shape[:-1] + (weight.shape[1],))


def attend(queries, key_rows, value_rows, seq_first):
    full_shape = queries.shape
    split_shape = full_shape[:-1] + (HEADS, HEAD)
    query_heads = queries.reshape(split_shape)
    key_heads = key_rows.reshape(split_shape)
    value_heads = value_rows.reshape(split_shape)
    if seq_first:
        score_form = "lbhe,kbhe->bhlk"
        weigh_form = "bhlk,kbhe->lbhe"
    else:
        score_form = "blhe,bkhe->bhlk"
        weigh_form = "bhlk,bkhe->blhe"
    scores = jnp.einsum(
        score_form, query_heads, key_heads, preferred_element_type=jnp.float32
    ) * HEAD ** (-0.5)
    probs = jax.nn.softmax(scores, axis=-1).astype(jnp.bfloat16)
    mixture = jnp.einsum(weigh_form, probs, value_heads, preferred_element_type=jnp.float32)
    return mixture.astype(jnp.bfloat16).reshape(full_shape)


def transformer_layer(tokens, weights, seq_first):
    qkv_weight, out_weight, up_weight, down_weight = weights
    model_width = tokens.shape[-1]
    normed = layer_norm(tokens).astype(jnp.bfloat16)
    triple = project(normed, qkv_weight).astype(jnp.bfloat16)
    attended = attend(
        triple[..., :model_width],
        triple[..., model_width : 2 * model_width],
        triple[..., 2 * model_width :],
        seq_first,
    )
    after_attention = rounded(tokens.astype(jnp.float32) + project(attended, out_weight))
    normed_again = layer_norm(after_attention).astype(jnp.bfloat16)
    hidden = jax.nn.relu(project(normed_again, up_weight)).astype(jnp.bfloat16)
    return (after_attention.astype(jnp.float32) + project(hidden, down_weight)).astype(jnp.bfloat16)


def encode(framed, enc_weight):
    return rounded(
        jax.nn.relu(
            jnp.dot(
                framed,
                enc_weight,
                precision=lax.Precision.HIGHEST,
                preferred_element_type=jnp.float32,
            )
        )
    )


def local(
    waveform,
    enc_weight,
    intra_qkv,
    intra_out,
    intra_up,
    intra_down,
    inter_qkv,
    inter_out,
    inter_up,
    inter_down,
    mask_weight,
):
    model_width = enc_weight.shape[1]
    frames_here = waveform.shape[0] // HOP
    blocks = waveform.reshape(frames_here, HOP)
    first_block = shifted(blocks[:1], "tm", -1)
    following = jnp.concatenate([blocks[1:], first_block], axis=0)
    framed = jnp.concatenate([blocks, following], axis=1)
    encoded = encode(framed, enc_weight)
    frame_edge = shifted(encoded[:HALF], "tm", -1)
    padded = jnp.concatenate([encoded, frame_edge], axis=0)
    segment_total = frames_here // HALF
    stacked = padded.reshape(segment_total + 1, HALF, model_width)
    segmented = jnp.concatenate([stacked[:-1], stacked[1:]], axis=1)
    intra_weights = (intra_qkv, intra_out, intra_up, intra_down)
    inter_weights = (inter_qkv, inter_out, inter_up, inter_down)
    within = transformer_layer(segmented, intra_weights, False)
    within = within.reshape(segment_total, 2, HALF, model_width)
    pieces = lax.all_to_all(within, "tm", split_axis=2, concat_axis=0, tiled=True)
    row_total, item_count, spot_count, feature_count = pieces.shape
    flattened = pieces.reshape(row_total, item_count * spot_count, feature_count)
    result = transformer_layer(flattened, inter_weights, True)
    across = result.reshape(row_total, item_count, spot_count, feature_count)
    returned = lax.all_to_all(across, "tm", split_axis=0, concat_axis=2, tiled=True)
    tail_half = shifted(returned[-1:, 1], "tm", 1)
    lagged = jnp.concatenate([tail_half, returned[:-1, 1]], axis=0)
    combined = rounded(returned[:, 0].astype(jnp.float32) + lagged.astype(jnp.float32))
    combined = combined.reshape(frames_here, model_width)
    activated = combined.astype(jnp.float32)
    activated = jnp.where(activated > 0, activated, 0.25 * activated).astype(jnp.bfloat16)
    mask_values = jax.nn.relu(jnp.dot(activated, mask_weight, preferred_element_type=jnp.float32))
    mask_values = mask_values.reshape(frames_here, 2, model_width)
    separated = (mask_values * encoded.astype(jnp.float32)[:, None, :]).astype(jnp.bfloat16)
    return jnp.transpose(separated, (1, 0, 2))


def split_three(values):
    high = values.astype(jnp.bfloat16)
    rest = values - high.astype(jnp.float32)
    middle = rest.astype(jnp.bfloat16)
    low = (rest - middle.astype(jnp.float32)).astype(jnp.bfloat16)
    return high, middle, low


def normalise(values, centre_ref, mean_ref):
    centred = dot(values, centre_ref[...])
    spread = dot((centred * centred).astype(jnp.bfloat16), mean_ref[...])
    scale = lax.rsqrt(spread + 1e-05)
    sides = [
        (centred[:, at : at + LANES] * scale).astype(jnp.bfloat16) for at in range(0, centred.shape[1], LANES)
    ]
    return jnp.concatenate(sides, axis=1)


def dot(left, right):
    return jnp.dot(left, right, preferred_element_type=jnp.float32)


def dot_nt(left, right):
    return lax.dot_general(left, right, (((1,), (1,)), ((), ())), preferred_element_type=jnp.float32)


def head_of(shape, axis):
    return lax.broadcasted_iota(jnp.int32, shape, axis) // HEAD


def by_head(queries):
    lanes = head_of(queries.shape, 1)
    zero = jnp.zeros_like(queries)
    return [jnp.where(lanes == h, queries, zero) for h in range(queries.shape[1] // HEAD)]


def feed_forward(tokens, attended, out_ref, up_ref, down_ref, centre_ref, mean_ref):
    after = (tokens + dot(attended, out_ref[...])).astype(jnp.bfloat16)
    hidden = jnp.maximum(dot(normalise(after, centre_ref, mean_ref), up_ref[...]), 0.0).astype(jnp.bfloat16)
    return (after + dot(hidden, down_ref[...])).astype(jnp.bfloat16).astype(jnp.float32)


SCORE_SCALE = math.log2(math.e) * HEAD ** (-0.5)
GROUP = 64
BATCH = 8
LANES = 128
NEAR = LANES // HEAD


def encode_chunk(c, wave_ref, stacked_weight, enc_ref, normed_ref, centre_ref, mean_ref):
    taps = wave_ref[c]
    count = taps.shape[1] - LANES
    following = pltpu.roll(taps, taps.shape[1] - 1, 1)
    high, middle, low = split_three(jnp.concatenate([taps[:, :count], following[:, :count]], axis=0))
    pad = jnp.zeros((32, count), jnp.bfloat16)
    stacked = jnp.concatenate([high, high, middle, high, low, middle, pad], axis=0)
    frames = lax.dot_general(
        stacked, stacked_weight, (((0,), (0,)), ((), ())), preferred_element_type=jnp.float32
    )
    encoded = jnp.maximum(frames, 0.0).astype(jnp.bfloat16)
    at = pl.ds(pl.multiple_of(c * count, count), count)
    enc_ref[at, :] = encoded
    normed_ref[at, :] = normalise(encoded, centre_ref, mean_ref)


def stack_weight(weight):
    high, middle, low = split_three(weight)
    pad = jnp.zeros((32, weight.shape[1]), jnp.bfloat16)
    return jnp.concatenate([high, middle, high, low, high, middle, pad], axis=0)


def intra_group(g, place, enc_ref, normed_ref, u_ref, pn_ref, key_ref, value_ref, within_ref, qkv_ref, out_ref, up_ref, down_ref, centre_ref, mean_ref):
    width = enc_ref.shape[1]
    start = pl.multiple_of(16 * (place // 2), 16)
    odd = place % 2 == 1
    picked = []
    for b in range(GROUP + 1):
        rows = enc_ref[pl.ds(pl.multiple_of((GROUP * g + b) * HALF + start, 16), 16), :].astype(jnp.float32)
        picked.append(jnp.where(odd, rows[8:], rows[:8]))
    tokens = jnp.concatenate(
        [half for b in range(GROUP) for half in (picked[b], picked[b + 1])], axis=0
    )
    queries = (dot(normalise(tokens.astype(jnp.bfloat16), centre_ref, mean_ref), qkv_ref[:, :width]) * SCORE_SCALE).astype(jnp.bfloat16)
    for part in range(width // LANES):
        at = slice(part * LANES, (part + 1) * LANES)
        for h, own in enumerate(by_head(queries[:, at])):
            u_ref[part * NEAR + h] = dot(own, key_ref[at, :]).astype(jnp.bfloat16)

    @pl.loop(0, GROUP // BATCH)
    def _(i):
        spans = [pl.ds(pl.multiple_of((i * BATCH + s) * 16, 16), 16) for s in range(BATCH)]
        spots = [
            pl.ds(pl.multiple_of((GROUP * g + i * BATCH + s) * HALF, HALF), 2 * HALF) for s in range(BATCH)
        ]
        scores = [
            dot_nt(u_ref[:, spans[s], :].reshape(16 * HEADS, width), normed_ref[spots[s], :])
            for s in range(BATCH)
        ]
        tops = [jnp.max(each, axis=-1, keepdims=True) for each in scores]
        probs = [jnp.exp2(each - top).astype(jnp.bfloat16) for each, top in zip(scores, tops)]
        mixed = [dot(probs[s], normed_ref[spots[s], :]) for s in range(BATCH)]
        means = dot(jnp.concatenate(probs, axis=0), mean_ref[...])
        for s in range(BATCH):
            inverse = (1.0 / width) / means[s * 16 * HEADS : (s + 1) * 16 * HEADS]
            scaled = [
                (mixed[s][:, at : at + LANES] * inverse).astype(jnp.bfloat16) for at in range(0, width, LANES)
            ]
            pn_ref[:, spans[s], :] = jnp.concatenate(scaled, axis=1).reshape(HEADS, 16, width)

    sides = []
    for part in range(width // LANES):
        side = dot(pn_ref[part * NEAR], value_ref[part * NEAR])
        for h in range(part * NEAR + 1, (part + 1) * NEAR):
            side += dot(pn_ref[h], value_ref[h])
        sides.append(side.astype(jnp.bfloat16))
    result = feed_forward(tokens, jnp.concatenate(sides, axis=1), out_ref, up_ref, down_ref, centre_ref, mean_ref)
    at = pl.ds(pl.multiple_of(g * GROUP * 16, GROUP * 16), GROUP * 16)
    for part in range(width // LANES):
        within_ref[part, at, :] = result[:, part * LANES : (part + 1) * LANES]


def inter_pair(t, segments, within_ref, qkv_ref, out_ref, up_ref, down_ref, centre_ref, mean_ref):
    width = qkv_ref.shape[0]
    sides = range(width // LANES)
    places = [(spot, half) for spot in range(2) for half in range(2)]
    tokens = jnp.concatenate(
        [
            jnp.concatenate(
                [
                    within_ref.at[part][pl.ds(2 * t + spot + 8 * half, segments, stride=16), :]
                    for part in sides
                ],
                axis=1,
            )
            for spot, half in places
        ],
        axis=0,
    )
    triple = dot(normalise(tokens.astype(jnp.bfloat16), centre_ref, mean_ref), qkv_ref[...])
    queries = (triple[:, :width] * SCORE_SCALE).astype(jnp.bfloat16)
    keys = triple[:, width : 2 * width].astype(jnp.bfloat16)
    values = triple[:, 2 * width :].astype(jnp.bfloat16)
    lanes = head_of((segments, LANES), 1)
    columns = []
    for part in sides:
        wide = slice(part * LANES, (part + 1) * LANES)
        rows = [slice(p * segments, (p + 1) * segments) for p in range(len(places))]
        scores = [
            dot_nt(jnp.concatenate(by_head(queries[at, wide]), axis=0), keys[at, wide]) for at in rows
        ]
        probs = [
            jnp.exp2(each - jnp.max(each, axis=-1, keepdims=True)).astype(jnp.bfloat16) for each in scores
        ]
        ones = jnp.ones((segments, LANES), jnp.bfloat16)
        mixed = [
            dot(each, jnp.concatenate([values[at, wide], ones], axis=1)) for each, at in zip(probs, rows)
        ]
        parts = []
        for each in mixed:
            chosen = each[:segments]
            for h in range(1, NEAR):
                head = each[h * segments : (h + 1) * segments]
                chosen = jnp.concatenate(
                    [jnp.where(lanes == h, head[:, at : at + LANES], chosen[:, at : at + LANES]) for at in (0, LANES)],
                    axis=1,
                )
            attended = chosen[:, :LANES] / chosen[:, LANES:]
            parts.append(attended.astype(jnp.bfloat16))
        columns.append(jnp.concatenate(parts, axis=0))
    across = feed_forward(tokens, jnp.concatenate(columns, axis=1), out_ref, up_ref, down_ref, centre_ref, mean_ref)
    row = lax.broadcasted_iota(jnp.int32, (segments, width), 0)
    results = []
    for spot in range(2):
        first = across[2 * spot * segments : (2 * spot + 1) * segments]
        second = across[(2 * spot + 1) * segments : (2 * spot + 2) * segments]
        lagged = jnp.where(row == 0, 0.0, pltpu.roll(second, 1, 0))
        combined = (first + lagged).astype(jnp.bfloat16).astype(jnp.float32)
        results.append(jnp.where(combined > 0, combined, 0.25 * combined))
    return results


def prepare(normed_ref, enc_ref, key_ref, value_ref, qkv_ref, centre_ref, mean_ref):
    width = qkv_ref.shape[0]
    tail = normed_ref.shape[0] - HALF
    normed_ref[tail:, :] = jnp.zeros((HALF, width), jnp.bfloat16)
    enc_ref[tail:, :] = jnp.zeros((HALF, width), jnp.bfloat16)
    row, column = (lax.broadcasted_iota(jnp.int32, centre_ref.shape, axis) for axis in range(2))
    centre_ref[...] = (jnp.where(row == column, 1.0, 0.0) - 1.0 / width).astype(jnp.bfloat16)
    mean_ref[...] = jnp.full(mean_ref.shape, 1.0 / width, jnp.bfloat16)
    key_ref[...] = qkv_ref[:, width : 2 * width].astype(jnp.float32).T.astype(jnp.bfloat16)
    for part in range(width // LANES):
        start = 2 * width + part * LANES
        for h, own in enumerate(by_head(qkv_ref[:, start : start + LANES])):
            value_ref[part * NEAR + h] = own


def layers_kernel(
    devices,
    taps_ref, enc_weight_ref,
    qkv_ref, out_ref, up_ref, down_ref,
    inter_qkv_ref, inter_out_ref, inter_up_ref, inter_down_ref,
    active_ref, own_ref,
    wave_ref, halo_ref, enc_ref, normed_ref, u_ref, pn_ref, key_ref, value_ref, within_ref,
    send_ref, landed_ref, centre_ref, mean_ref,
    halo_sems, wave_sent, wave_landed, rows_sent, rows_landed,
):
    place = lax.axis_index("tm")
    count, width = own_ref.shape
    segments = devices * count // HALF
    stages = send_ref.shape[0]
    blocks = count // HALF

    def peer(k, sign):
        far = (place // 4 + sign * (k // 4) + devices) % (devices // 4)
        return far * 4 + (place // 2 + k // 2) % 2 * 2 + (place + k) % 2

    barrier = pltpu.get_barrier_semaphore()

    @pl.loop(1, devices)
    def _(k):
        pl.semaphore_signal(barrier, inc=1, device_id={"tm": peer(k, 1)}, device_id_type=pl.DeviceIdType.MESH)

    pl.semaphore_wait(barrier, devices - 1)
    halo = pltpu.make_async_remote_copy(
        src_ref=taps_ref.at[:, pl.ds(0, LANES)],
        dst_ref=halo_ref,
        send_sem=halo_sems.at[0],
        recv_sem=halo_sems.at[1],
        device_id={"tm": (place + devices - 1) % devices},
        device_id_type=pl.DeviceIdType.MESH,
    )
    halo.start()
    prepare(normed_ref, enc_ref, key_ref, value_ref, qkv_ref, centre_ref, mean_ref)
    stacked_weight = stack_weight(enc_weight_ref[...])
    wave_ref[place, :, :count] = taps_ref[...]
    halo.wait()
    wave_ref[place, :, count:] = jnp.where(place < devices - 1, halo_ref[...], 0.0)

    def wave_copy(k, slot):
        return pltpu.make_async_remote_copy(
            src_ref=wave_ref.at[slot],
            dst_ref=wave_ref.at[slot],
            send_sem=wave_sent.at[k],
            recv_sem=wave_landed.at[k],
            device_id={"tm": peer(k, 1)},
            device_id_type=pl.DeviceIdType.MESH,
        )

    @pl.loop(1, devices)
    def _(k):
        wave_copy(k, place).start()

    encode_chunk(place, wave_ref, stacked_weight, enc_ref, normed_ref, centre_ref, mean_ref)
    own_ref[...] = enc_ref[pl.ds(pl.multiple_of(place * count, count), count), :]

    @pl.loop(1, devices)
    def _(k):
        source = peer(k, -1)
        wave_copy(k, source).wait_recv()
        encode_chunk(source, wave_ref, stacked_weight, enc_ref, normed_ref, centre_ref, mean_ref)

    @pl.loop(1, devices)
    def _(k):
        wave_copy(k, place).wait_send()

    @pl.loop(0, segments // GROUP)
    def _(g):
        intra_group(g, place, enc_ref, normed_ref, u_ref, pn_ref, key_ref, value_ref, within_ref, qkv_ref, out_ref, up_ref, down_ref, centre_ref, mean_ref)

    def rows_copy(t, k, slot):
        return pltpu.make_async_remote_copy(
            src_ref=send_ref.at[t, peer(k, 1)],
            dst_ref=landed_ref.at[slot, t],
            send_sem=rows_sent.at[t, k],
            recv_sem=rows_landed.at[t, k],
            device_id={"tm": peer(k, 1)},
            device_id_type=pl.DeviceIdType.MESH,
        )

    @pl.loop(0, stages)
    def _(t):
        pair = inter_pair(t, segments, within_ref, inter_qkv_ref, inter_out_ref, inter_up_ref, inter_down_ref, centre_ref, mean_ref)
        pair = [each.reshape(devices, blocks, width) for each in pair]
        send_ref[t] = jnp.concatenate(pair, axis=1).astype(jnp.bfloat16)
        landed_ref[place, t] = send_ref[t, place]

        @pl.loop(1, devices)
        def _(k):
            rows_copy(t, devices - k, place).start()

    @pl.loop(0, stages)
    def _(t):
        @pl.loop(1, devices)
        def _(k):
            rows_copy(t, k, peer(k, -1)).wait_recv()

    for source in range(devices):
        for t in range(stages):
            rows = landed_ref[source, t].astype(jnp.float32)
            for spot in range(2):
                for part in range(width // LANES):
                    at = pl.ds(2 * stages * source + 2 * t + spot, blocks, stride=HALF)
                    within_ref.at[part][at, :] = rows[
                        spot * blocks : (spot + 1) * blocks, part * LANES : (part + 1) * LANES
                    ]
    for part in range(width // LANES):
        active_ref[:, part * LANES : (part + 1) * LANES] = within_ref[part, :count, :].astype(jnp.bfloat16)

    @pl.loop(0, stages)
    def _(t):
        @pl.loop(1, devices)
        def _(k):
            rows_copy(t, k, place).wait_send()


def mask_kernel(active_ref, encoded_ref, mask_ref, result_ref):
    rows, width = encoded_ref.shape
    step = rows // 4
    for part in range(4):
        at = slice(part * step, (part + 1) * step)
        encoded = encoded_ref[at, :].astype(jnp.float32)
        for speaker in range(2):
            values = dot(active_ref[at, :], mask_ref[:, speaker * width : (speaker + 1) * width])
            result_ref[speaker, at, :] = (jnp.maximum(values, 0.0) * encoded).astype(jnp.bfloat16)


def local_positions(
    waveform, enc_weight, intra_qkv, intra_out, intra_up, intra_down,
    inter_qkv, inter_out, inter_up, inter_down, mask_weight,
):
    width = enc_weight.shape[1]
    devices = lax.axis_size("tm")
    here = waveform.shape[0] // HOP
    frames = here * devices
    segments = frames // HALF
    stages = HALF // devices // 2
    blocks = here // HALF
    taps = waveform.reshape(here, HOP).T
    vmem = pl.BlockSpec(memory_space=pltpu.VMEM)
    half = jnp.bfloat16
    active, encoded = pl.pallas_call(
        functools.partial(layers_kernel, devices),
        out_shape=(jax.ShapeDtypeStruct((here, width), half), jax.ShapeDtypeStruct((here, width), half)),
        in_specs=[vmem] * 10,
        out_specs=(vmem, vmem),
        scratch_shapes=[
            pltpu.VMEM((devices, HOP, here + LANES), jnp.float32),
            pltpu.VMEM((HOP, LANES), jnp.float32),
            pltpu.VMEM((frames + HALF, width), half),
            pltpu.VMEM((frames + HALF, width), half),
            pltpu.VMEM((HEADS, GROUP * 16, width), half),
            pltpu.VMEM((HEADS, GROUP * 16, width), half),
            pltpu.VMEM((width, width), half),
            pltpu.VMEM((HEADS, width, LANES), half),
            pltpu.VMEM((width // LANES, segments * 16, LANES), jnp.float32),
            pltpu.VMEM((stages, devices, 2 * blocks, width), half),
            pltpu.VMEM((devices, stages, 2 * blocks, width), half),
            pltpu.VMEM((width, width), half),
            pltpu.VMEM((width, LANES), half),
            pltpu.SemaphoreType.DMA((2,)),
            pltpu.SemaphoreType.DMA((devices,)),
            pltpu.SemaphoreType.DMA((devices,)),
            pltpu.SemaphoreType.DMA((stages, devices)),
            pltpu.SemaphoreType.DMA((stages, devices)),
        ],
        compiler_params=pltpu.CompilerParams(
            vmem_limit_bytes=56 * 1024 * 1024, collective_id=0, has_side_effects=True
        ),
        name="layers",
    )(taps, enc_weight, intra_qkv, intra_out, intra_up, intra_down, inter_qkv, inter_out, inter_up, inter_down)
    return pl.pallas_call(
        mask_kernel,
        out_shape=jax.ShapeDtypeStruct((2, here, width), half),
        in_specs=[vmem] * 3,
        out_specs=vmem,
        compiler_params=pltpu.CompilerParams(vmem_limit_bytes=24 * 1024 * 1024),
        name="mask",
    )(active, encoded, mask_weight)


def solution(mesh):
    body = local_positions if mesh.shape["tm"] * 8 == HALF else local
    return jax.shard_map(
        body,
        mesh=mesh,
        in_specs=(P(("grp", "tm")), P(), P(), P(), P(), P(), P(), P(), P(), P(), P()),
        out_specs=P(None, ("grp", "tm"), None),
        check_vma=False,
    )
```

```python
import functools
import math

import jax
import jax.numpy as jnp
from jax import lax
from jax.experimental import pallas as pl
from jax.experimental.pallas import tpu as pltpu
from jax.sharding import PartitionSpec as P

HEADS = 8
HEAD = 32
HOP = 8
HALF = 128


def shifted(value, axis, steps):
    count = lax.axis_size(axis)
    leading, last = (max(0, -steps), min(count, count - steps))
    return lax.ppermute(value, axis, [(source, source + steps) for source in range(leading, last)])


def rounded(values):
    return lax.optimization_barrier(values.astype(jnp.bfloat16))


def layer_norm(values):
    values = values.astype(jnp.float32)
    centred = values - jnp.mean(values, axis=-1, keepdims=True)
    spread = jnp.mean(centred * centred, axis=-1, keepdims=True)
    return centred * lax.rsqrt(spread + 1e-05)


def project(values, weight):
    flattened = values.reshape(-1, values.shape[-1])
    result = jnp.dot(flattened, weight, preferred_element_type=jnp.float32)
    return result.reshape(values.shape[:-1] + (weight.shape[1],))


def attend(queries, key_rows, value_rows, seq_first):
    full_shape = queries.shape
    split_shape = full_shape[:-1] + (HEADS, HEAD)
    query_heads = queries.reshape(split_shape)
    key_heads = key_rows.reshape(split_shape)
    value_heads = value_rows.reshape(split_shape)
    if seq_first:
        score_form = "lbhe,kbhe->bhlk"
        weigh_form = "bhlk,kbhe->lbhe"
    else:
        score_form = "blhe,bkhe->bhlk"
        weigh_form = "bhlk,bkhe->blhe"
    scores = jnp.einsum(
        score_form, query_heads, key_heads, preferred_element_type=jnp.float32
    ) * HEAD ** (-0.5)
    probs = jax.nn.softmax(scores, axis=-1).astype(jnp.bfloat16)
    mixture = jnp.einsum(weigh_form, probs, value_heads, preferred_element_type=jnp.float32)
    return mixture.astype(jnp.bfloat16).reshape(full_shape)


def transformer_layer(tokens, weights, seq_first):
    qkv_weight, out_weight, up_weight, down_weight = weights
    model_width = tokens.shape[-1]
    normed = layer_norm(tokens).astype(jnp.bfloat16)
    triple = project(normed, qkv_weight).astype(jnp.bfloat16)
    attended = attend(
        triple[..., :model_width],
        triple[..., model_width : 2 * model_width],
        triple[..., 2 * model_width :],
        seq_first,
    )
    after_attention = rounded(tokens.astype(jnp.float32) + project(attended, out_weight))
    normed_again = layer_norm(after_attention).astype(jnp.bfloat16)
    hidden = jax.nn.relu(project(normed_again, up_weight)).astype(jnp.bfloat16)
    return (after_attention.astype(jnp.float32) + project(hidden, down_weight)).astype(jnp.bfloat16)


def encode(framed, enc_weight):
    return rounded(
        jax.nn.relu(
            jnp.dot(
                framed,
                enc_weight,
                precision=lax.Precision.HIGHEST,
                preferred_element_type=jnp.float32,
            )
        )
    )


def local(
    waveform,
    enc_weight,
    intra_qkv,
    intra_out,
    intra_up,
    intra_down,
    inter_qkv,
    inter_out,
    inter_up,
    inter_down,
    mask_weight,
):
    model_width = enc_weight.shape[1]
    frames_here = waveform.shape[0] // HOP
    blocks = waveform.reshape(frames_here, HOP)
    first_block = shifted(blocks[:1], "tm", -1)
    following = jnp.concatenate([blocks[1:], first_block], axis=0)
    framed = jnp.concatenate([blocks, following], axis=1)
    encoded = encode(framed, enc_weight)
    frame_edge = shifted(encoded[:HALF], "tm", -1)
    padded = jnp.concatenate([encoded, frame_edge], axis=0)
    segment_total = frames_here // HALF
    stacked = padded.reshape(segment_total + 1, HALF, model_width)
    segmented = jnp.concatenate([stacked[:-1], stacked[1:]], axis=1)
    intra_weights = (intra_qkv, intra_out, intra_up, intra_down)
    inter_weights = (inter_qkv, inter_out, inter_up, inter_down)
    within = transformer_layer(segmented, intra_weights, False)
    within = within.reshape(segment_total, 2, HALF, model_width)
    pieces = lax.all_to_all(within, "tm", split_axis=2, concat_axis=0, tiled=True)
    row_total, item_count, spot_count, feature_count = pieces.shape
    flattened = pieces.reshape(row_total, item_count * spot_count, feature_count)
    result = transformer_layer(flattened, inter_weights, True)
    across = result.reshape(row_total, item_count, spot_count, feature_count)
    returned = lax.all_to_all(across, "tm", split_axis=0, concat_axis=2, tiled=True)
    tail_half = shifted(returned[-1:, 1], "tm", 1)
    lagged = jnp.concatenate([tail_half, returned[:-1, 1]], axis=0)
    combined = rounded(returned[:, 0].astype(jnp.float32) + lagged.astype(jnp.float32))
    combined = combined.reshape(frames_here, model_width)
    activated = combined.astype(jnp.float32)
    activated = jnp.where(activated > 0, activated, 0.25 * activated).astype(jnp.bfloat16)
    mask_values = jax.nn.relu(jnp.dot(activated, mask_weight, preferred_element_type=jnp.float32))
    mask_values = mask_values.reshape(frames_here, 2, model_width)
    separated = (mask_values * encoded.astype(jnp.float32)[:, None, :]).astype(jnp.bfloat16)
    return jnp.transpose(separated, (1, 0, 2))


def split_three(values):
    high = values.astype(jnp.bfloat16)
    rest = values - high.astype(jnp.float32)
    middle = rest.astype(jnp.bfloat16)
    low = (rest - middle.astype(jnp.float32)).astype(jnp.bfloat16)
    return high, middle, low


def skewed(items, stages):
    items = list(items)
    for step in range(len(items) + len(stages) - 1):
        for depth, stage in enumerate(stages):
            at = step - depth
            if 0 <= at < len(items):
                items[at] = stage(items[at])
    return items


def centre(values, centre_ref):
    return dot(values, centre_ref[...])


def rescale(centred, mean_ref):
    spread = dot((centred * centred).astype(jnp.bfloat16), mean_ref[...])
    scale = lax.rsqrt(spread + 1e-05)
    sides = [
        (centred[:, at : at + LANES] * scale).astype(jnp.bfloat16) for at in range(0, centred.shape[1], LANES)
    ]
    return jnp.concatenate(sides, axis=1)


def tiles(total, size):
    return [slice(at, at + size) for at in range(0, total, size)]


def normalise(values, centre_ref, mean_ref):
    parts = skewed(
        [values[at] for at in tiles(values.shape[0], 128)],
        [lambda each: centre(each, centre_ref), lambda each: rescale(each, mean_ref)],
    )
    return jnp.concatenate(parts, axis=0)


def dot(left, right):
    return jnp.dot(left, right, preferred_element_type=jnp.float32)


def dot_nt(left, right):
    return lax.dot_general(left, right, (((1,), (1,)), ((), ())), preferred_element_type=jnp.float32)


def head_of(shape, axis):
    return lax.broadcasted_iota(jnp.int32, shape, axis) // HEAD


def by_head(queries):
    lanes = head_of(queries.shape, 1)
    zero = jnp.zeros_like(queries)
    return [jnp.where(lanes == h, queries, zero) for h in range(queries.shape[1] // HEAD)]


def feed_forward(tokens, attended, out_ref, up_ref, down_ref, centre_ref, mean_ref):
    def project(at):
        return (tokens[at] + dot(attended[at], out_ref[...])).astype(jnp.bfloat16)

    def open_norm(after):
        return after, centre(after, centre_ref)

    def close_norm(state):
        return state[0], rescale(state[1], mean_ref)

    def widen(state):
        return state[0], jnp.maximum(dot(state[1], up_ref[...]), 0.0).astype(jnp.bfloat16)

    def narrow(state):
        total = state[0].astype(jnp.float32) + dot(state[1], down_ref[...])
        return total.astype(jnp.bfloat16).astype(jnp.float32)

    parts = skewed(tiles(tokens.shape[0], 128), [project, open_norm, close_norm, widen, narrow])
    return jnp.concatenate(parts, axis=0)


SCORE_SCALE = math.log2(math.e) * HEAD ** (-0.5)
GROUP = 64
BATCH = 16
LANES = 128
NEAR = LANES // HEAD


def encode_chunk(c, wave_ref, stacked_weight, enc_ref, normed_ref, centre_ref, mean_ref):
    taps = wave_ref[c]
    count = taps.shape[1] - LANES
    following = pltpu.roll(taps, taps.shape[1] - 1, 1)
    high, middle, low = split_three(jnp.concatenate([taps[:, :count], following[:, :count]], axis=0))
    pad = jnp.zeros((32, count), jnp.bfloat16)
    stacked = jnp.concatenate([high, high, middle, high, low, middle, pad], axis=0)
    def product(at):
        frames = lax.dot_general(
            stacked[:, at], stacked_weight, (((0,), (0,)), ((), ())), preferred_element_type=jnp.float32
        )
        return at, jnp.maximum(frames, 0.0).astype(jnp.bfloat16)

    def open_norm(state):
        at, encoded = state
        rows = pl.ds(pl.multiple_of(c * count + at.start, HALF), HALF)
        enc_ref[rows, :] = encoded
        return rows, centre(encoded, centre_ref)

    def close_norm(state):
        rows, centred = state
        normed_ref[rows, :] = rescale(centred, mean_ref)

    skewed(tiles(count, HALF), [product, open_norm, close_norm])


def stack_weight(weight):
    high, middle, low = split_three(weight)
    pad = jnp.zeros((32, weight.shape[1]), jnp.bfloat16)
    return jnp.concatenate([high, middle, high, low, high, middle, pad], axis=0)


def intra_group(g, place, enc_ref, normed_ref, u_ref, pn_ref, key_ref, value_ref, within_ref, qkv_ref, out_ref, up_ref, down_ref, centre_ref, mean_ref):
    width = enc_ref.shape[1]
    start = pl.multiple_of(16 * (place // 2), 16)
    odd = place % 2 == 1
    picked = []
    for b in range(GROUP + 1):
        rows = enc_ref[pl.ds(pl.multiple_of((GROUP * g + b) * HALF + start, 16), 16), :].astype(jnp.float32)
        picked.append(jnp.where(odd, rows[8:], rows[:8]))
    tokens = jnp.concatenate(
        [half for b in range(GROUP) for half in (picked[b], picked[b + 1])], axis=0
    )
    queries = (dot(normalise(tokens.astype(jnp.bfloat16), centre_ref, mean_ref), qkv_ref[:, :width]) * SCORE_SCALE).astype(jnp.bfloat16)
    for part in range(width // LANES):
        at = slice(part * LANES, (part + 1) * LANES)
        for h, own in enumerate(by_head(queries[:, at])):
            u_ref[part * NEAR + h] = dot(own, key_ref[at, :]).astype(jnp.bfloat16)

    @pl.loop(0, GROUP // BATCH)
    def _(i):
        spans = [pl.ds(pl.multiple_of((i * BATCH + s) * 16, 16), 16) for s in range(BATCH)]
        spots = [
            pl.ds(pl.multiple_of((GROUP * g + i * BATCH + s) * HALF, HALF), 2 * HALF) for s in range(BATCH)
        ]

        def score(n):
            return n, dot_nt(u_ref[:, spans[n], :].reshape(16 * HEADS, width), normed_ref[spots[n], :])

        def soften(state):
            n, scores = state
            probs = jnp.exp2(scores - jnp.max(scores, axis=-1, keepdims=True))
            return n, probs.astype(jnp.bfloat16), 1.0 / jnp.sum(probs, axis=-1, keepdims=True)

        def mix(state):
            n, probs, inverse = state
            mixed = dot(probs, normed_ref[spots[n], :]) * inverse
            pn_ref[:, spans[n], :] = mixed.astype(jnp.bfloat16).reshape(HEADS, 16, width)

        skewed(range(BATCH), [score, soften, mix])

    sides = []
    for part in range(width // LANES):
        side = dot(pn_ref[part * NEAR], value_ref[part * NEAR])
        for h in range(part * NEAR + 1, (part + 1) * NEAR):
            side += dot(pn_ref[h], value_ref[h])
        sides.append(side.astype(jnp.bfloat16))
    result = feed_forward(tokens, jnp.concatenate(sides, axis=1), out_ref, up_ref, down_ref, centre_ref, mean_ref)
    at = pl.ds(pl.multiple_of(g * GROUP * 16, GROUP * 16), GROUP * 16)
    for part in range(width // LANES):
        within_ref[part, at, :] = result[:, part * LANES : (part + 1) * LANES]


def inter_pair(t, segments, within_ref, qkv_ref, out_ref, up_ref, down_ref, centre_ref, mean_ref):
    width = qkv_ref.shape[0]
    sides = range(width // LANES)
    places = [(spot, half) for spot in range(2) for half in range(2)]
    tokens = jnp.concatenate(
        [
            jnp.concatenate(
                [
                    within_ref.at[part][pl.ds(2 * t + spot + 8 * half, segments, stride=16), :]
                    for part in sides
                ],
                axis=1,
            )
            for spot, half in places
        ],
        axis=0,
    )
    triple = dot(normalise(tokens.astype(jnp.bfloat16), centre_ref, mean_ref), qkv_ref[...])
    queries = (triple[:, :width] * SCORE_SCALE).astype(jnp.bfloat16)
    keys = triple[:, width : 2 * width].astype(jnp.bfloat16)
    values = triple[:, 2 * width :].astype(jnp.bfloat16)
    lanes = head_of((segments, LANES), 1)
    ones = jnp.ones((segments, LANES), jnp.bfloat16)

    def score(item):
        wide = slice(item[0] * LANES, (item[0] + 1) * LANES)
        rows = slice(item[1] * segments, (item[1] + 1) * segments)
        scores = dot_nt(jnp.concatenate(by_head(queries[rows, wide]), axis=0), keys[rows, wide])
        return scores, jnp.concatenate([values[rows, wide], ones], axis=1)

    def soften(state):
        scores, extended = state
        return jnp.exp2(scores - jnp.max(scores, axis=-1, keepdims=True)).astype(jnp.bfloat16), extended

    def mix(state):
        mixed = dot(*state)
        top, total = mixed[:segments, :LANES], mixed[:segments, LANES:]
        for h in range(1, NEAR):
            head = mixed[h * segments : (h + 1) * segments]
            top = jnp.where(lanes == h, head[:, :LANES], top)
            total = jnp.where(lanes == h, head[:, LANES:], total)
        return (top / total).astype(jnp.bfloat16)

    count = len(places)
    parts = skewed([(part, place) for part in sides for place in range(count)], [score, soften, mix])
    columns = [jnp.concatenate(parts[part * count : (part + 1) * count], axis=0) for part in sides]
    across = feed_forward(tokens, jnp.concatenate(columns, axis=1), out_ref, up_ref, down_ref, centre_ref, mean_ref)
    row = lax.broadcasted_iota(jnp.int32, (segments, width), 0)
    results = []
    for spot in range(2):
        first = across[2 * spot * segments : (2 * spot + 1) * segments]
        second = across[(2 * spot + 1) * segments : (2 * spot + 2) * segments]
        lagged = jnp.where(row == 0, 0.0, pltpu.roll(second, 1, 0))
        combined = (first + lagged).astype(jnp.bfloat16).astype(jnp.float32)
        results.append(jnp.where(combined > 0, combined, 0.25 * combined))
    return results


def prepare(normed_ref, enc_ref, key_ref, value_ref, qkv_ref, centre_ref, mean_ref):
    width = qkv_ref.shape[0]
    tail = normed_ref.shape[0] - HALF
    normed_ref[tail:, :] = jnp.zeros((HALF, width), jnp.bfloat16)
    enc_ref[tail:, :] = jnp.zeros((HALF, width), jnp.bfloat16)
    row, column = (lax.broadcasted_iota(jnp.int32, centre_ref.shape, axis) for axis in range(2))
    centre_ref[...] = (jnp.where(row == column, 1.0, 0.0) - 1.0 / width).astype(jnp.bfloat16)
    mean_ref[...] = jnp.full(mean_ref.shape, 1.0 / width, jnp.bfloat16)
    key_ref[...] = qkv_ref[:, width : 2 * width].astype(jnp.float32).T.astype(jnp.bfloat16)
    for part in range(width // LANES):
        start = 2 * width + part * LANES
        for h, own in enumerate(by_head(qkv_ref[:, start : start + LANES])):
            value_ref[part * NEAR + h] = own


def layers_kernel(
    devices,
    taps_ref, enc_weight_ref,
    qkv_ref, out_ref, up_ref, down_ref,
    inter_qkv_ref, inter_out_ref, inter_up_ref, inter_down_ref,
    active_ref, own_ref,
    wave_ref, halo_ref, enc_ref, normed_ref, u_ref, pn_ref, key_ref, value_ref, within_ref,
    send_ref, landed_ref, centre_ref, mean_ref,
    halo_sems, wave_sent, wave_landed, rows_sent, rows_landed,
):
    place = lax.axis_index("tm")
    count, width = own_ref.shape
    segments = devices * count // HALF
    stages = send_ref.shape[0]
    blocks = count // HALF

    def peer(k, sign):
        far = (place // 4 + sign * (k // 4) + devices) % (devices // 4)
        return far * 4 + (place // 2 + k // 2) % 2 * 2 + (place + k) % 2

    barrier = pltpu.get_barrier_semaphore()

    @pl.loop(1, devices)
    def _(k):
        pl.semaphore_signal(barrier, inc=1, device_id={"tm": peer(k, 1)}, device_id_type=pl.DeviceIdType.MESH)

    pl.semaphore_wait(barrier, devices - 1)
    halo = pltpu.make_async_remote_copy(
        src_ref=taps_ref.at[:, pl.ds(0, LANES)],
        dst_ref=halo_ref,
        send_sem=halo_sems.at[0],
        recv_sem=halo_sems.at[1],
        device_id={"tm": (place + devices - 1) % devices},
        device_id_type=pl.DeviceIdType.MESH,
    )
    halo.start()
    prepare(normed_ref, enc_ref, key_ref, value_ref, qkv_ref, centre_ref, mean_ref)
    stacked_weight = stack_weight(enc_weight_ref[...])
    wave_ref[place, :, :count] = taps_ref[...]
    halo.wait()
    wave_ref[place, :, count:] = jnp.where(place < devices - 1, halo_ref[...], 0.0)

    planes = devices // 4
    far, near, core = place // 4, place // 2 % 2, place % 2
    across_y = far * 4 + (1 - near) * 2 + core
    across_core = far * 4 + near * 2 + 1 - core

    def wave_copy(k, slot, target):
        return pltpu.make_async_remote_copy(
            src_ref=wave_ref.at[slot],
            dst_ref=wave_ref.at[slot],
            send_sem=wave_sent.at[k],
            recv_sem=wave_landed.at[k],
            device_id={"tm": target},
            device_id_type=pl.DeviceIdType.MESH,
        )

    def chunk(step, side_y, side_core):
        plane = (far - step + planes) % planes
        return plane * 4 + (near + side_y) % 2 * 2 + (core + side_core) % 2

    def encode_here(slot):
        encode_chunk(slot, wave_ref, stacked_weight, enc_ref, normed_ref, centre_ref, mean_ref)

    @pl.loop(1, planes)
    def _(step):
        wave_copy(step, place, (far + step) % planes * 4 + near * 2 + core).start()

    wave_copy(planes, place, across_y).start()
    wave_copy(2 * planes, place, across_core).start()
    encode_here(place)
    own_ref[...] = enc_ref[pl.ds(pl.multiple_of(place * count, count), count), :]

    @pl.loop(1, planes)
    def _(step):
        slot = chunk(step, 0, 0)
        wave_copy(step, slot, across_y).wait_recv()
        wave_copy(planes + step, slot, across_y).start()
        wave_copy(2 * planes + step, slot, across_core).start()
        encode_here(slot)

    @pl.loop(0, planes)
    def _(step):
        slot = chunk(step, 1, 0)
        wave_copy(planes + step, slot, across_y).wait_recv()
        wave_copy(3 * planes + step, slot, across_core).start()
        encode_here(slot)

    @pl.loop(0, 2 * planes)
    def _(step):
        slot = chunk(step % planes, step // planes, 1)
        wave_copy(2 * planes + step, slot, across_core).wait_recv()
        encode_here(slot)

    @pl.loop(1, 4 * planes)
    def _(k):
        wave_copy(k, place, across_core).wait_send()

    @pl.loop(0, segments // GROUP)
    def _(g):
        intra_group(g, place, enc_ref, normed_ref, u_ref, pn_ref, key_ref, value_ref, within_ref, qkv_ref, out_ref, up_ref, down_ref, centre_ref, mean_ref)

    def rows_copy(t, k, slot):
        return pltpu.make_async_remote_copy(
            src_ref=send_ref.at[t, peer(k, 1)],
            dst_ref=landed_ref.at[slot, t],
            send_sem=rows_sent.at[t, k],
            recv_sem=rows_landed.at[t, k],
            device_id={"tm": peer(k, 1)},
            device_id_type=pl.DeviceIdType.MESH,
        )

    @pl.loop(0, stages)
    def _(t):
        pair = inter_pair(t, segments, within_ref, inter_qkv_ref, inter_out_ref, inter_up_ref, inter_down_ref, centre_ref, mean_ref)
        pair = [each.reshape(devices, blocks, width) for each in pair]
        send_ref[t] = jnp.concatenate(pair, axis=1).astype(jnp.bfloat16)
        landed_ref[place, t] = send_ref[t, place]

        @pl.loop(1, devices)
        def _(k):
            rows_copy(t, devices - k, place).start()

    @pl.loop(0, stages)
    def _(t):
        @pl.loop(1, devices)
        def _(k):
            rows_copy(t, k, peer(k, -1)).wait_recv()

    for source in range(devices):
        for t in range(stages):
            rows = landed_ref[source, t].astype(jnp.float32)
            for spot in range(2):
                for part in range(width // LANES):
                    at = pl.ds(2 * stages * source + 2 * t + spot, blocks, stride=HALF)
                    within_ref.at[part][at, :] = rows[
                        spot * blocks : (spot + 1) * blocks, part * LANES : (part + 1) * LANES
                    ]
    for part in range(width // LANES):
        active_ref[:, part * LANES : (part + 1) * LANES] = within_ref[part, :count, :].astype(jnp.bfloat16)

    @pl.loop(0, stages)
    def _(t):
        @pl.loop(1, devices)
        def _(k):
            rows_copy(t, k, place).wait_send()


def mask_kernel(active_ref, encoded_ref, mask_ref, result_ref):
    rows, width = encoded_ref.shape
    step = rows // 4
    for part in range(4):
        at = slice(part * step, (part + 1) * step)
        encoded = encoded_ref[at, :].astype(jnp.float32)
        for speaker in range(2):
            values = dot(active_ref[at, :], mask_ref[:, speaker * width : (speaker + 1) * width])
            result_ref[speaker, at, :] = (jnp.maximum(values, 0.0) * encoded).astype(jnp.bfloat16)


def local_positions(
    waveform, enc_weight, intra_qkv, intra_out, intra_up, intra_down,
    inter_qkv, inter_out, inter_up, inter_down, mask_weight,
):
    width = enc_weight.shape[1]
    devices = lax.axis_size("tm")
    here = waveform.shape[0] // HOP
    frames = here * devices
    segments = frames // HALF
    stages = HALF // devices // 2
    blocks = here // HALF
    taps = waveform.reshape(here, HOP).T
    vmem = pl.BlockSpec(memory_space=pltpu.VMEM)
    half = jnp.bfloat16
    active, encoded = pl.pallas_call(
        functools.partial(layers_kernel, devices),
        out_shape=(jax.ShapeDtypeStruct((here, width), half), jax.ShapeDtypeStruct((here, width), half)),
        in_specs=[vmem] * 10,
        out_specs=(vmem, vmem),
        scratch_shapes=[
            pltpu.VMEM((devices, HOP, here + LANES), jnp.float32),
            pltpu.VMEM((HOP, LANES), jnp.float32),
            pltpu.VMEM((frames + HALF, width), half),
            pltpu.VMEM((frames + HALF, width), half),
            pltpu.VMEM((HEADS, GROUP * 16, width), half),
            pltpu.VMEM((HEADS, GROUP * 16, width), half),
            pltpu.VMEM((width, width), half),
            pltpu.VMEM((HEADS, width, LANES), half),
            pltpu.VMEM((width // LANES, segments * 16, LANES), jnp.float32),
            pltpu.VMEM((stages, devices, 2 * blocks, width), half),
            pltpu.VMEM((devices, stages, 2 * blocks, width), half),
            pltpu.VMEM((width, width), half),
            pltpu.VMEM((width, LANES), half),
            pltpu.SemaphoreType.DMA((2,)),
            pltpu.SemaphoreType.DMA((devices,)),
            pltpu.SemaphoreType.DMA((devices,)),
            pltpu.SemaphoreType.DMA((stages, devices)),
            pltpu.SemaphoreType.DMA((stages, devices)),
        ],
        compiler_params=pltpu.CompilerParams(
            vmem_limit_bytes=56 * 1024 * 1024, collective_id=0, has_side_effects=True
        ),
        name="layers",
    )(taps, enc_weight, intra_qkv, intra_out, intra_up, intra_down, inter_qkv, inter_out, inter_up, inter_down)
    return pl.pallas_call(
        mask_kernel,
        out_shape=jax.ShapeDtypeStruct((2, here, width), half),
        in_specs=[vmem] * 3,
        out_specs=vmem,
        compiler_params=pltpu.CompilerParams(vmem_limit_bytes=24 * 1024 * 1024),
        name="mask",
    )(active, encoded, mask_weight)


def solution(mesh):
    body = local_positions if mesh.shape["tm"] * 8 == HALF else local
    return jax.shard_map(
        body,
        mesh=mesh,
        in_specs=(P(("grp", "tm")), P(), P(), P(), P(), P(), P(), P(), P(), P(), P()),
        out_specs=P(None, ("grp", "tm"), None),
        check_vma=False,
    )
```
